32 devices in a mesh: dp: 4 (over y, x), ctx: 8 (over z, core).
Axes of the slice: x: 2, y: 2, z: 4, core: 2. Of those that a mesh axis runs over, the one named last changes fastest.
Arguments:
- residual: bfloat16 [4, 1024, 4096], P('dp', 'ctx'), may hold values from -6 to 6
- queries: bfloat16 [4, 1024, 512], P('dp', 'ctx'), may hold values from -6 to 6
- keys_values: bfloat16 [4, 1024, 256], P('dp', 'ctx'), may hold values from -6 to 6
- out_grad: bfloat16 [4, 1024, 512], P('dp', 'ctx'), may hold values from -12 to 12
- w_out: bfloat16 [512, 4096], replicated, may hold values from -0.25 to 0.25
- norm_gain: float32 [4096], replicated, may hold values from 0.5 to 2
- w_router: bfloat16 [4096, 32], replicated, may hold values from -0.09375 to 0.09375
- expert_ids: int32 [4, 1024, 8], P('dp', 'ctx'), may hold values from 0 to 31, all different within a row; in each aligned block of 128 rows (0 to 127, 128 to 255, ..., all dimensions but the last counted through in order) at most 34 rows name the same one
- w_gate_up: bfloat16 [32, 4096, 1536], P(('dp', 'ctx')), may hold values from -0.09375 to 0.09375
- w_down: bfloat16 [32, 768, 4096], P(('dp', 'ctx')), may hold values from -0.21875 to 0.21875
Outputs:
- layer_out: bfloat16 [4, 1024, 4096], P('dp', 'ctx')
- query_grad: bfloat16 [4, 1024, 512], P('dp', 'ctx')
- pair_grad: float32 [4, 1024, 256], P('dp', 'ctx')
The draws below stay inside these ranges and needn't reach their ends.
Inputs may be any that keep to these rules, and one draw needn't show every extreme that they name: `expert_ids`: within the 128 tokens of one device (aligned blocks of tokens, sequences in order), no expert is named by more than 34 of the choices, a bound that some block reaches. The 8 experts of a token differ.
All inputs are finite; a program needn't handle non-finite values.
Results may differ from the reference program's by a relative error of at most 0.03.
Values may be sent and summed in bfloat16 or wider, within the bound.
A program may use at most 192 MiB of HBM per device.

```python
import math
import jax
import jax.numpy as jnp
import numpy as np
from jax import lax

D = 4096
HD = 128
TOPK = 8
HQ = 4
FFW = 768
TOK_DEV = 128
SEQS = 4
LEN = 1024
EXPERTS = 32
CAP = 34
N_DP = 4
N_CTX = 8


def paired_draw(key):
    query_key = jax.random.fold_in(key, 101)
    pair_key = jax.random.fold_in(key, 102)
    query_shape = (SEQS, LEN, HQ * HD)
    pair_shape = (SEQS, LEN, 2 * HD)
    query_vals = jnp.clip(jax.random.normal(query_key, query_shape, jnp.float32), -6.0, 6.0)
    pair_vals = jnp.clip(jax.random.normal(pair_key, pair_shape, jnp.float32), -6.0, 6.0)
    return (query_vals, pair_vals)


def draw_queries(key, part):
    return paired_draw(key)[0].astype(jnp.bfloat16)


def draw_keys_values(key, part):
    return paired_draw(key)[1].astype(jnp.bfloat16)


def levels(key, extent, cuts, least, largest):
    def one(axis_at, shards_of):
        steps = jax.random.uniform(jax.random.fold_in(jax.random.fold_in(key, 6), axis_at), (shards_of,), jnp.float32, least / len(cuts), largest / len(cuts))
        return jnp.repeat(jnp.exp(steps), extent[axis_at] // shards_of).reshape((-1,) + (1,) * (len(extent) - axis_at - 1))

    gain = one(*cuts[0])
    for cut in cuts[1:]:
        gain = gain * one(*cut)
    return gain


def assign_block(own_key, own, number, rows, amount, top, reach, slope):
    order = jax.random.permutation(own_key, amount)
    heavy_load, common = portions_of(amount, rows * top, reach, slope, True), portions_of(amount, rows * top, reach, slope, False)
    places = jnp.arange(amount)

    def named(sizes, turn):
        used = int((sizes > 0).sum())
        fixed = max(1, used // 4)
        passed = fixed + (places - fixed + turn * (used - fixed)) % max(1, amount - fixed)
        return jnp.zeros((amount,), jnp.int32).at[order[jnp.where(places < fixed, places, passed)]].set(jnp.asarray(sizes, jnp.int32))

    sizes = jnp.where(number % 4 == 0, named(heavy_load, number // 4), named(common, number - number // 4 - 1))
    mixed = jax.random.permutation(jax.random.fold_in(own, 3), amount)
    source_of, receiver = mixed[0:amount // 2 * 2:2], mixed[1:amount // 2 * 2:2]
    slack = jnp.minimum(sizes[source_of] - 1, reach - sizes[receiver]) // 2
    slack = jnp.where((source_of == order[0]) | (receiver == order[0]) | (sizes[receiver] == 0), 0, jnp.maximum(slack, 0))
    passed = jax.random.randint(jax.random.fold_in(own, 4), (amount // 2,), 0, 1 << 20) % (slack + 1)
    sizes = sizes.at[source_of].add(-passed).at[receiver].add(passed)
    labels = jnp.searchsorted(jnp.cumsum(sizes), jnp.arange(rows * top), side="right").astype(jnp.int32)
    listing = labels.reshape(top, rows).T
    listing = listing[jax.random.permutation(jax.random.fold_in(own, 1), rows)]
    turn = jax.random.randint(jax.random.fold_in(own, 2), (rows, 1), 0, top)
    return jnp.take_along_axis(listing, (jnp.arange(top)[None, :] + turn) % top, axis=1)


def portions_of(amount, total, most, lean, full):
    weights = [(1 << 20) // math.isqrt(standing ** lean) + 1 for standing in range(1, amount + 1)]
    largest = most if full else min(most, max(-(-total // amount), total * weights[0] // sum(weights)))
    least = 1 if total - largest >= amount - 1 else 0
    given, surplus = [largest] + [least] * (amount - 1), total - largest - least * (amount - 1)
    while surplus > 0:
        candidates = [i for i in range(1, amount) if given[i] < largest] or [i for i in range(1, amount) if given[i] < most]
        whole, remaining = sum([weights[i] for i in candidates]), surplus
        for i in candidates:
            addition = min(most - given[i], max(1, remaining * weights[i] // whole), surplus)
            given[i] = given[i] + addition
            surplus = surplus - addition
    return np.array(given)


def centred(stream_key, shape, spread, bound, shards=(), kind=jnp.bfloat16):
    entries = jax.random.normal(stream_key, shape, jnp.float32) * spread
    if len(shards) > 0:
        entries = levels(stream_key, shape, shards, -0.22, 0.18) * entries
    return jnp.clip(entries, min=-bound, max=bound).astype(kind)


def setup_inputs(seed: int = 0) -> dict:
    keys = jax.random.split(jax.random.key(seed), 11)
    residual = centred(keys[0], (SEQS, LEN, D), 1.0, 6.0, ((0, 4), (1, 8)))
    queries = draw_queries(jax.random.fold_in(keys[10], 71), 0)
    keys_values = draw_keys_values(jax.random.fold_in(keys[10], 71), 0)
    out_grad = centred(keys[3], (SEQS, LEN, HQ * HD), 2.0, 12.0, ((0, 4), (1, 8)))
    w_out = centred(keys[4], (HQ * HD, D), (HQ * HD) ** -0.5, 0.25)
    norm_gain = jnp.clip(jnp.exp(jax.random.uniform(keys[5], (D,), jnp.float32, math.log(0.5), math.log(2.0))), 0.5, 2.0)
    w_router = centred(keys[6], (D, EXPERTS), D ** -0.5, 0.09375)
    expert_ids_keys = jax.random.split(jax.random.fold_in(keys[7], 1), SEQS * LEN // TOK_DEV)
    expert_ids_turns = jax.random.permutation(jax.random.fold_in(keys[7], 3), SEQS * LEN // TOK_DEV)
    expert_ids = jax.vmap(lambda own, number: assign_block(jax.random.fold_in(keys[7], 2), own, number, TOK_DEV, EXPERTS, TOPK, CAP, 2))(expert_ids_keys, expert_ids_turns).reshape((SEQS, LEN, TOPK))
    w_gate_up = centred(keys[8], (EXPERTS, D, 2 * FFW), D ** -0.5, 0.09375, ((0, 32),))
    w_down = centred(keys[9], (EXPERTS, FFW, D), FFW ** -0.5, 0.21875, ((0, 32),))
    return {"residual": residual, "queries": queries, "keys_values": keys_values, "out_grad": out_grad, "w_out": w_out, "norm_gain": norm_gain, "w_router": w_router, "expert_ids": expert_ids, "w_gate_up": w_gate_up, "w_down": w_down}


norm_eps = 1e-06

def attend(operands):
    queries, keys_values, out_grad = operands
    length = queries.shape[0]
    head_rows = queries.reshape(length, HQ, HD).astype(jnp.float32)
    key_rows = keys_values[:, :HD].astype(jnp.float32)
    value_rows = keys_values[:, HD:].astype(jnp.float32)
    factor = HD ** (-0.5)
    highest_prec = lax.Precision.HIGHEST
    scores = jnp.einsum('qhd,kd->hqk', head_rows, key_rows, precision=highest_prec) * factor
    positions = jnp.arange(length)
    causal = positions[None, :] <= positions[:, None]
    scores = jnp.where(causal[None], scores, -jnp.inf)
    highest = lax.optimization_barrier(jnp.max(scores, axis=-1, keepdims=True))
    weights = jnp.exp(scores - highest)
    attn_probs = weights / lax.optimization_barrier(jnp.sum(weights, axis=-1, keepdims=True))
    probs_low = attn_probs.astype(jnp.bfloat16)
    probs_wide = probs_low.astype(jnp.float32)
    attended = jnp.einsum('hqk,kd->qhd', probs_wide, value_rows, precision=highest_prec).astype(jnp.bfloat16)
    cotangent = out_grad.reshape(length, HQ, HD).astype(jnp.float32)
    row_dot = lax.optimization_barrier(jnp.sum(cotangent * attended.astype(jnp.float32), axis=-1))
    prob_grad = jnp.einsum('qhd,kd->hqk', cotangent, value_rows, precision=highest_prec)
    score_grad = (attn_probs * (prob_grad - row_dot.T[:, :, None])).astype(jnp.bfloat16)
    score_wide = score_grad.astype(jnp.float32)
    query_grad = (factor * jnp.einsum('hqk,kd->qhd', score_wide, key_rows, precision=highest_prec)).astype(jnp.bfloat16)
    key_grad = factor * jnp.einsum('hqk,qhd->kd', score_wide, head_rows, precision=highest_prec)
    value_grad = jnp.einsum('hqk,qhd->kd', probs_wide, cotangent, precision=highest_prec)
    return (attended.reshape(length, HQ * HD), query_grad.reshape(length, HQ * HD), jnp.concatenate([key_grad, value_grad], axis=1))

def reference(residual, queries, keys_values, out_grad, w_out, norm_gain, w_router, expert_ids, w_gate_up, w_down):
    attended, query_grad, pair_grad = lax.map(attend, (queries, keys_values, out_grad))
    token_count = SEQS * LEN
    hidden = residual.reshape(token_count, D).astype(jnp.float32) + jnp.dot(attended.reshape(token_count, HQ * HD), w_out, preferred_element_type=jnp.float32)
    normed = (hidden * lax.rsqrt(lax.optimization_barrier(jnp.mean(hidden * hidden, axis=-1, keepdims=True)) + norm_eps) * norm_gain).astype(jnp.bfloat16)
    logits = jnp.dot(normed, w_router, preferred_element_type=jnp.float32)
    choice_rows = expert_ids.reshape(token_count, TOPK)
    chosen = jnp.take_along_axis(logits, choice_rows, axis=1)
    gate_values = jax.nn.sigmoid(chosen)
    mixing = (gate_values / lax.optimization_barrier(jnp.sum(gate_values, axis=-1, keepdims=True))).reshape(-1)
    routed = choice_rows.reshape(-1)
    slot_count = N_DP * N_CTX * CAP
    hidden_width = w_down.shape[1]

    def one_expert(running, expert):
        member = routed == expert
        picked = jnp.nonzero(member, size=slot_count, fill_value=0)[0].astype(jnp.int32)
        live_rows = (jnp.arange(slot_count) < jnp.sum(member.astype(jnp.int32))).astype(jnp.float32)
        token_rows = picked // TOPK
        inputs = normed[token_rows].astype(jnp.float32)
        gate_up = jnp.dot(inputs, w_gate_up[expert].astype(jnp.float32), precision=lax.Precision.HIGHEST)
        active = (jax.nn.silu(gate_up[:, :hidden_width]) * gate_up[:, hidden_width:]).astype(jnp.bfloat16)
        result = jnp.dot(active.astype(jnp.float32), w_down[expert].astype(jnp.float32), precision=lax.Precision.HIGHEST).astype(jnp.bfloat16)
        scaled = result.astype(jnp.float32) * (mixing[picked] * live_rows)[:, None]
        return (running.at[token_rows].add(scaled), None)
    mixture, unused = lax.scan(one_expert, jnp.zeros((token_count, D), jnp.float32), jnp.arange(EXPERTS, dtype=jnp.int32))
    layer_out = (hidden + mixture).astype(jnp.bfloat16).reshape(SEQS, LEN, D)
    return (layer_out, query_grad, pair_grad)
```

```python
import jax
import jax.numpy as jnp
from jax import lax
from jax.sharding import PartitionSpec as P

D = 4096
HD = 128
TOPK = 8
HQ = 4


norm_eps = 1e-06


def expert_block(arrived, w_gate_up, w_down):
    hidden_width = w_down.shape[1]
    gate_up = jnp.einsum("sjid,jdf->sjif", arrived, w_gate_up, preferred_element_type=jnp.float32)
    active = (jax.nn.silu(gate_up[..., :hidden_width]) * gate_up[..., hidden_width:]).astype(
        jnp.bfloat16
    )
    return jnp.einsum("sjif,jfd->sjid", active, w_down, preferred_element_type=jnp.float32).astype(
        jnp.bfloat16
    )


def exchange_mixture(normed, routed, mixing, route_match, w_gate_up, w_down):
    tokens_dev, experts_all = normed.shape[0], route_match.shape[2]
    capacity = tokens_dev * TOPK // experts_all + 2
    onehot = route_match.reshape(tokens_dev * TOPK, experts_all).astype(jnp.int32)
    before = jnp.cumsum(onehot, axis=0) - onehot
    ranked = jnp.sum(before * onehot, axis=1)
    slot_index = routed.reshape(-1) * capacity + ranked
    repeated = jnp.repeat(normed, TOPK, axis=0)
    outgoing = jnp.zeros((experts_all * capacity, D), jnp.bfloat16).at[slot_index].set(repeated)
    dp_size = lax.axis_size("dp")
    ctx_size = lax.axis_size("ctx")
    per_dev = w_gate_up.shape[0]
    returned = lax.all_to_all(
        expert_block(
            lax.all_to_all(
                outgoing.reshape(dp_size * ctx_size, per_dev, capacity, D),
                ("dp", "ctx"),
                split_axis=0,
                concat_axis=0,
                tiled=True,
            ),
            w_gate_up,
            w_down,
        ),
        ("dp", "ctx"),
        split_axis=0,
        concat_axis=0,
        tiled=True,
    )
    results = returned.reshape(experts_all * capacity, D)[slot_index]
    mixture = jnp.einsum(
        "tk,tkd->td", mixing, results.reshape(tokens_dev, TOPK, D).astype(jnp.float32)
    )
    return mixture


def gathered_mixture(normed, dense_mix, w_gate_up, w_down):
    tokens_dev, experts_all = dense_mix.shape
    hidden_width = w_down.shape[1]
    axes = ("dp", "ctx")
    blocks = lax.axis_size("dp") * lax.axis_size("ctx")
    capacity = tokens_dev * TOPK // experts_all + 2
    group = 4
    groups, group_rows, group_cap = blocks // group, group * tokens_dev, group * capacity
    rows_all = lax.all_gather(normed, axes, axis=0, tiled=True)
    weights = lax.all_to_all(
        dense_mix.T.reshape(experts_all, 1, tokens_dev), axes, split_axis=0, concat_axis=0, tiled=True
    ).reshape(groups, group_rows)
    named = weights != 0.0
    rank = jnp.cumsum(named.astype(jnp.int32), axis=1) - 1
    slots = jnp.arange(group_cap, dtype=jnp.int32)
    pick = (rank[:, None, :] == slots[None, :, None]) & named[:, None, :]
    slot_weight = jnp.sum(jnp.where(pick, weights[:, None, :], 0.0), axis=2)
    pick = pick.astype(jnp.bfloat16)
    arrived = jnp.einsum(
        "gct,gtd->gcd",
        pick,
        rows_all.reshape(groups, group_rows, D),
        preferred_element_type=jnp.float32,
    ).astype(jnp.bfloat16)
    arrived = arrived.reshape(groups * group_cap, D)
    gate_up = jnp.dot(arrived, w_gate_up[0], preferred_element_type=jnp.float32)
    active = (jax.nn.silu(gate_up[:, :hidden_width]) * gate_up[:, hidden_width:]).astype(
        jnp.bfloat16
    )
    outs = jnp.dot(active, w_down[0], preferred_element_type=jnp.float32).astype(jnp.bfloat16)
    outs = (outs.astype(jnp.float32) * slot_weight.reshape(-1, 1)).astype(jnp.bfloat16)
    part = jnp.einsum(
        "gct,gcd->gtd",
        pick,
        outs.reshape(groups, group_cap, D),
        preferred_element_type=jnp.float32,
    ).astype(jnp.bfloat16)
    return lax.psum_scatter(
        part.reshape(blocks * tokens_dev, D), axes, scatter_dimension=0, tiled=True
    ).astype(jnp.float32)


def shards(
    residual,
    queries,
    keys_values,
    out_grad,
    w_out,
    norm_gain,
    w_router,
    expert_ids,
    w_gate_up,
    w_down,
):
    tokens_dev = queries.shape[1]
    row_count = tokens_dev * HQ
    factor = HD ** (-0.5)
    head_rows = queries.reshape(row_count, HD)
    grad_rows = out_grad.reshape(row_count, HD)
    whole_pairs = lax.all_gather(keys_values, "ctx", axis=1, tiled=True)
    length = whole_pairs.shape[1]
    key_rows = whole_pairs[0, :, :HD]
    value_rows = whole_pairs[0, :, HD:]
    offset = lax.axis_index("ctx") * tokens_dev
    query_pos = offset + jnp.arange(row_count, dtype=jnp.int32) // HQ
    key_pos = jnp.arange(length, dtype=jnp.int32)
    causal = key_pos[None, :] <= query_pos[:, None]
    scores = (
        jnp.einsum("rd,kd->rk", head_rows, key_rows, preferred_element_type=jnp.float32) * factor
    )
    scores = jnp.where(causal, scores, -jnp.inf)
    highest = jnp.max(scores, axis=1, keepdims=True)
    weights = jnp.exp(scores - highest)
    totals = jnp.sum(weights, axis=1, keepdims=True)
    attn_probs = weights / totals
    probs_low = attn_probs.astype(jnp.bfloat16)
    attended = jnp.dot(probs_low, value_rows, preferred_element_type=jnp.float32).astype(
        jnp.bfloat16
    )
    row_dot = jnp.sum(
        grad_rows.astype(jnp.float32) * attended.astype(jnp.float32), axis=1, keepdims=True
    )
    prob_grad = jnp.einsum("rd,kd->rk", grad_rows, value_rows, preferred_element_type=jnp.float32)
    score_grad = (attn_probs * (prob_grad - row_dot)).astype(jnp.bfloat16)
    query_grad = (
        jnp.dot(score_grad, key_rows, preferred_element_type=jnp.float32) * factor
    ).astype(jnp.bfloat16)
    key_part = (
        jnp.einsum("rk,rd->kd", score_grad, head_rows, preferred_element_type=jnp.float32) * factor
    )
    value_part = jnp.einsum("rk,rd->kd", probs_low, grad_rows, preferred_element_type=jnp.float32)
    pair_grad = lax.psum_scatter(
        jnp.concatenate([key_part, value_part], axis=1).astype(jnp.bfloat16),
        "ctx",
        scatter_dimension=0,
        tiled=True,
    ).astype(jnp.float32)
    hidden = residual.reshape(tokens_dev, D).astype(jnp.float32) + jnp.dot(
        attended.reshape(tokens_dev, HQ * HD), w_out, preferred_element_type=jnp.float32
    )
    normed = (
        hidden * lax.rsqrt(jnp.mean(hidden * hidden, axis=1, keepdims=True) + norm_eps) * norm_gain
    ).astype(jnp.bfloat16)
    logits = jnp.dot(normed, w_router, preferred_element_type=jnp.float32)
    experts_all = w_router.shape[1]
    routed = expert_ids.reshape(tokens_dev, TOPK)
    route_match = routed[:, :, None] == jnp.arange(experts_all, dtype=jnp.int32)[None, None, :]
    chosen = jnp.sum(jnp.where(route_match, logits[:, None, :], 0.0), axis=2)
    gate_values = jax.nn.sigmoid(chosen)
    mixing = gate_values / jnp.sum(gate_values, axis=1, keepdims=True)
    if experts_all <= 4 * TOPK:
        dense_mix = jnp.sum(jnp.where(route_match, mixing[:, :, None], 0.0), axis=1)
        mixture = gathered_mixture(normed, dense_mix, w_gate_up, w_down)
    else:
        mixture = exchange_mixture(normed, routed, mixing, route_match, w_gate_up, w_down)
    layer_out = (hidden + mixture).astype(jnp.bfloat16).reshape(1, tokens_dev, D)
    return (
        layer_out,
        query_grad.reshape(1, tokens_dev, HQ * HD),
        pair_grad.reshape(1, tokens_dev, 2 * HD),
    )


def solution(mesh):
    placed = (
        P("dp", "ctx", None),
        P("dp", "ctx", None),
        P("dp", "ctx", None),
        P("dp", "ctx", None),
        P(),
        P(),
        P(),
        P("dp", "ctx", None),
        P(("dp", "ctx"), None, None),
        P(("dp", "ctx"), None, None),
    )
    return jax.shard_map(
        shards,
        mesh=mesh,
        in_specs=placed,
        out_specs=(P("dp", "ctx", None), P("dp", "ctx", None), P("dp", "ctx", None)),
        check_vma=False,
    )
```

```python
import functools

import jax
import jax.numpy as jnp
from jax import lax
from jax.experimental import pallas as pl
from jax.experimental.pallas import tpu as pltpu
from jax.sharding import PartitionSpec as P

D = 4096
HD = 128
TOPK = 8
HQ = 4


norm_eps = 1e-06


def expert_block(arrived, w_gate_up, w_down):
    hidden_width = w_down.shape[1]
    gate_up = jnp.einsum("sjid,jdf->sjif", arrived, w_gate_up, preferred_element_type=jnp.float32)
    active = (jax.nn.silu(gate_up[..., :hidden_width]) * gate_up[..., hidden_width:]).astype(
        jnp.bfloat16
    )
    return jnp.einsum("sjif,jfd->sjid", active, w_down, preferred_element_type=jnp.float32).astype(
        jnp.bfloat16
    )


def exchange_mixture(normed, routed, mixing, route_match, w_gate_up, w_down):
    tokens_dev, experts_all = normed.shape[0], route_match.shape[2]
    capacity = tokens_dev * TOPK // experts_all + 2
    onehot = route_match.reshape(tokens_dev * TOPK, experts_all).astype(jnp.int32)
    before = jnp.cumsum(onehot, axis=0) - onehot
    ranked = jnp.sum(before * onehot, axis=1)
    slot_index = routed.reshape(-1) * capacity + ranked
    repeated = jnp.repeat(normed, TOPK, axis=0)
    outgoing = jnp.zeros((experts_all * capacity, D), jnp.bfloat16).at[slot_index].set(repeated)
    dp_size = lax.axis_size("dp")
    ctx_size = lax.axis_size("ctx")
    per_dev = w_gate_up.shape[0]
    returned = lax.all_to_all(
        expert_block(
            lax.all_to_all(
                outgoing.reshape(dp_size * ctx_size, per_dev, capacity, D),
                ("dp", "ctx"),
                split_axis=0,
                concat_axis=0,
                tiled=True,
            ),
            w_gate_up,
            w_down,
        ),
        ("dp", "ctx"),
        split_axis=0,
        concat_axis=0,
        tiled=True,
    )
    results = returned.reshape(experts_all * capacity, D)[slot_index]
    mixture = jnp.einsum(
        "tk,tkd->td", mixing, results.reshape(tokens_dev, TOPK, D).astype(jnp.float32)
    )
    return mixture


MESH = pl.DeviceIdType.MESH


class Place:
    def __init__(self, depth):
        self.depth = depth
        self.dp = lax.axis_index("dp")
        ctx = lax.axis_index("ctx")
        self.z, self.core = ctx // 2, ctx % 2
        x_flip = (self.dp // 2) * 2 + 1 - self.dp % 2
        y_flip = (self.dp + 2) % 4
        self.near_dp = x_flip * (1 - self.core) + y_flip * self.core
        self.far_dp = y_flip * (1 - self.core) + x_flip * self.core
        self.both_dp = 3 - self.dp
        self.near = (self.near_dp, ctx)
        self.far = (self.far_dp, ctx)
        self.other_core = (self.dp, self.z * 2 + 1 - self.core)
        self.up = (self.dp, ctx + 2)
        self.down = (self.dp, ctx - 2)
        self.has_up = self.z < depth - 1
        self.has_down = self.z > 0

    def block(self, dp, z, core=None):
        return (dp * self.depth + z) * 2 + (self.core if core is None else core)

    def greet(self):
        barrier = pltpu.get_barrier_semaphore()
        for target in (self.near, self.far, self.other_core):
            pl.semaphore_signal(barrier, inc=1, device_id=target, device_id_type=MESH)

        @pl.when(self.has_up)
        def _():
            pl.semaphore_signal(barrier, inc=1, device_id=self.up, device_id_type=MESH)

        @pl.when(self.has_down)
        def _():
            pl.semaphore_signal(barrier, inc=1, device_id=self.down, device_id_type=MESH)

        pl.semaphore_wait(
            barrier, 3 + self.has_up.astype(jnp.int32) + self.has_down.astype(jnp.int32)
        )


def gather_kernel(depth, rows_ref, all_ref, own_sem, send_sem, recv_sem):
    place = Place(depth)
    z = place.z
    targets = (place.near, place.far, place.other_core, place.up, place.down)
    NEAR, FAR, CORE, UP, DOWN = range(5)
    own = place.block(place.dp, z)

    def copy(kind, block, source=None):
        return pltpu.make_async_remote_copy(
            src_ref=all_ref.at[block] if source is None else source,
            dst_ref=all_ref.at[block],
            send_sem=send_sem.at[kind, block],
            recv_sem=recv_sem.at[block],
            device_id=targets[kind],
            device_id_type=MESH,
        )

    def along(distance):
        if distance == 0:
            return [(z, None, None)]
        return [(z - distance, z >= distance, UP), (z + distance, z + distance < depth, DOWN)]

    def run(condition, body):
        if condition is None:
            body()
        else:
            pl.when(condition)(body)

    own_copy = pltpu.make_async_copy(rows_ref, all_ref.at[own], own_sem)
    place.greet()
    own_copy.start()
    pl.when(place.has_up)(lambda: copy(UP, own, rows_ref).start())
    pl.when(place.has_down)(lambda: copy(DOWN, own, rows_ref).start())
    for kind in (FAR, NEAR, CORE):
        copy(kind, own, rows_ref).start()

    def from_line(distance):
        for source, condition, onward in along(distance):

            def body(source=source, onward=onward):
                block = place.block(place.dp, source)
                copy(onward, block).wait_recv()
                more = place.has_up if onward == UP else place.has_down
                pl.when(more)(lambda: copy(onward, block).start())
                for kind in (NEAR, FAR, CORE):
                    copy(kind, block).start()

            run(condition, body)

    def from_near(distance):
        for source, condition, _ in along(distance):

            def body(source=source):
                block = place.block(place.near_dp, source)
                copy(NEAR, block).wait_recv()
                for kind in (FAR, CORE):
                    copy(kind, block).start()

            run(condition, body)

    def from_far(distance):
        for source, condition, _ in along(distance):

            def body(source=source):
                for dp in (place.far_dp, place.both_dp):
                    block = place.block(dp, source)
                    copy(FAR, block).wait_recv()
                    copy(CORE, block).start()

            run(condition, body)

    for distance in range(depth):
        if distance:
            from_line(distance)
        from_near(distance)
        if distance:
            from_far(distance - 1)
    from_far(depth - 1)

    for dp in range(4):
        for level in range(depth):
            copy(CORE, place.block(dp, level, 1 - place.core)).wait_recv()
    own_copy.wait()
    for distance in range(depth):
        for source, condition, onward in along(distance):

            def body(source=source, onward=onward):
                block = place.block(place.dp, source)
                for kind in (NEAR, FAR, CORE):
                    copy(kind, block).wait_send()
                if onward != DOWN:
                    pl.when(place.has_up)(lambda: copy(UP, block).wait_send())
                if onward != UP:
                    pl.when(place.has_down)(lambda: copy(DOWN, block).wait_send())
                block = place.block(place.near_dp, source)
                for kind in (FAR, CORE):
                    copy(kind, block).wait_send()
                for dp in (place.far_dp, place.both_dp):
                    copy(CORE, place.block(dp, source)).wait_send()

            run(condition, body)


def gather_rows(rows, depth):
    tokens_dev, width = rows.shape
    blocks = 8 * depth
    return pl.pallas_call(
        functools.partial(gather_kernel, depth),
        out_shape=jax.ShapeDtypeStruct((blocks, tokens_dev, width), rows.dtype),
        in_specs=[pl.BlockSpec(memory_space=pl.ANY)],
        out_specs=pl.BlockSpec(memory_space=pl.ANY),
        scratch_shapes=[
            pltpu.SemaphoreType.DMA(()),
            pltpu.SemaphoreType.DMA((5, blocks)),
            pltpu.SemaphoreType.DMA((blocks,)),
        ],
        compiler_params=pltpu.CompilerParams(collective_id=1, has_side_effects=True),
    )(rows)


def reduce_kernel(
    depth,
    part_ref,
    out_ref,
    total,
    core_in,
    far_in,
    near_in,
    line_in,
    own_sem,
    core_send,
    core_recv,
    far_send,
    far_recv,
    near_send,
    near_recv,
    line_send,
    line_recv,
):
    place = Place(depth)
    z = place.z
    rows = out_ref.shape[0]

    def order(i):
        falling = lambda at: jnp.where(
            depth - 1 - i > at, depth - 1 - i, depth - 2 - i if i < depth - 1 else at
        )
        return jnp.where(z < depth // 2, falling(z), depth - 1 - falling(depth - 1 - z))

    levels = [order(i) for i in range(depth)]

    def add(into, term):
        def step(i, carry):
            at = pl.ds(pl.multiple_of(i * 16, 16), 16)
            into[at, :] = (
                into[at, :].astype(jnp.float32) + term[at, :].astype(jnp.float32)
            ).astype(jnp.bfloat16)
            return carry

        lax.fori_loop(0, rows // 16, step, 0)

    def remote(source, into, send, recv, target):
        return pltpu.make_async_remote_copy(
            src_ref=source,
            dst_ref=into,
            send_sem=send,
            recv_sem=recv,
            device_id=target,
            device_id_type=MESH,
        )

    def slot(dp, level):
        return dp * depth + level

    def load(dp, level):
        at = slot(dp, level)
        return pltpu.make_async_copy(
            part_ref.at[place.block(dp, level)], total.at[at], own_sem.at[at]
        )

    def to_core(dp, level):
        at = slot(dp, level)
        return remote(
            part_ref.at[place.block(dp, level, 1 - place.core)],
            core_in.at[at],
            core_send.at[at],
            core_recv.at[at],
            place.other_core,
        )

    def to_far(side, dp, level):
        at = side * depth + level
        return remote(
            total.at[slot(dp, level)], far_in.at[at], far_send.at[at], far_recv.at[at], place.far
        )

    def to_near(level):
        return remote(
            total.at[slot(place.near_dp, level)],
            near_in.at[level],
            near_send.at[level],
            near_recv.at[level],
            place.near,
        )

    def to_line(level, at, target):
        return remote(
            total.at[slot(place.dp, level)],
            line_in.at[at],
            line_send.at[level],
            line_recv.at[at],
            target,
        )

    place.greet()
    theirs = (place.both_dp, place.near_dp, place.far_dp, place.dp)
    mine = (place.both_dp, place.far_dp, place.near_dp, place.dp)
    for dp in range(4):
        for level in levels:
            to_core(theirs[dp], level).start()
            load(mine[dp], level).start()
    for turn, dp in enumerate(mine):
        for level in levels:
            at = slot(dp, level)
            load(dp, level).wait()
            to_core(dp, level).wait_recv()
            add(total.at[at], core_in.at[at])
            if turn < 2:
                to_far(1 - turn, dp, level).start()
    for level in levels:
        at = slot(place.near_dp, level)
        to_far(1, place.both_dp, level).wait_recv()
        add(total.at[at], far_in.at[depth + level])
        to_near(level).start()
    for level in levels:
        at = slot(place.dp, level)
        to_far(0, place.far_dp, level).wait_recv()
        add(total.at[at], far_in.at[level])
        to_near(level).wait_recv()
        add(total.at[at], near_in.at[level])

        @pl.when(level > z)
        def _():
            @pl.when(place.has_down)
            def _():
                to_line(level, level, place.up).wait_recv()
                add(total.at[at], line_in.at[level])

            to_line(level, level, place.up).start()

        @pl.when(level < z)
        def _():
            @pl.when(place.has_up)
            def _():
                to_line(level, level, place.down).wait_recv()
                add(total.at[at], line_in.at[level])

            to_line(level, jnp.where(level == z - 1, depth, level), place.down).start()

    at = slot(place.dp, z)

    @pl.when(place.has_down)
    def _():
        to_line(z, z, place.up).wait_recv()
        add(total.at[at], line_in.at[z])

    @pl.when(place.has_up)
    def _():
        to_line(z, depth, place.down).wait_recv()
        add(total.at[at], line_in.at[depth])

    out_ref[...] = total[at]

    for dp in range(4):
        for level in levels:
            to_core(theirs[dp], level).wait_send()
    for level in levels:
        to_far(1, place.both_dp, level).wait_send()
        to_far(0, place.far_dp, level).wait_send()
        to_near(level).wait_send()

        @pl.when(level != z)
        def _():
            to_line(level, level, place.up).wait_send()


def reduce_rows(part, depth):
    blocks, tokens_dev, width = part.shape
    half = blocks // 2

    def buffer(count):
        return pltpu.VMEM((count, tokens_dev, width), part.dtype)

    def sems(count):
        return pltpu.SemaphoreType.DMA((count,))

    return pl.pallas_call(
        functools.partial(reduce_kernel, depth),
        out_shape=jax.ShapeDtypeStruct((tokens_dev, width), part.dtype),
        in_specs=[pl.BlockSpec(memory_space=pl.ANY)],
        out_specs=pl.BlockSpec(memory_space=pltpu.VMEM),
        scratch_shapes=[
            buffer(half),
            buffer(half),
            buffer(2 * depth),
            buffer(depth),
            buffer(depth + 1),
            sems(half),
            sems(half),
            sems(half),
            sems(2 * depth),
            sems(2 * depth),
            sems(depth),
            sems(depth),
            sems(depth),
            sems(depth + 1),
        ],
        compiler_params=pltpu.CompilerParams(
            collective_id=2, has_side_effects=True, vmem_limit_bytes=60 * 2**20
        ),
    )(part)


def gathered_mixture(normed, dense_mix, w_gate_up, w_down):
    tokens_dev, experts_all = dense_mix.shape
    hidden_width = w_down.shape[1]
    axes = ("dp", "ctx")
    blocks = lax.axis_size("dp") * lax.axis_size("ctx")
    capacity = tokens_dev * TOPK // experts_all + 2
    group = 4
    groups, group_rows, group_cap = blocks // group, group * tokens_dev, group * capacity
    depth = lax.axis_size("ctx") // 2
    rows_all = gather_rows(normed, depth)
    weights = lax.all_to_all(
        dense_mix.T.reshape(experts_all, 1, tokens_dev), axes, split_axis=0, concat_axis=0, tiled=True
    ).reshape(groups, group_rows)
    named = weights != 0.0
    rank = jnp.cumsum(named.astype(jnp.int32), axis=1) - 1
    slots = jnp.arange(group_cap, dtype=jnp.int32)
    pick = (rank[:, None, :] == slots[None, :, None]) & named[:, None, :]
    slot_weight = jnp.sum(jnp.where(pick, weights[:, None, :], 0.0), axis=2)
    pick = pick.astype(jnp.bfloat16)
    arrived = jnp.einsum(
        "gct,gtd->gcd",
        pick,
        rows_all.reshape(groups, group_rows, D),
        preferred_element_type=jnp.float32,
    ).astype(jnp.bfloat16)
    arrived = arrived.reshape(groups * group_cap, D)
    gate_up = jnp.dot(arrived, w_gate_up[0], preferred_element_type=jnp.float32)
    active = (jax.nn.silu(gate_up[:, :hidden_width]) * gate_up[:, hidden_width:]).astype(
        jnp.bfloat16
    )
    outs = jnp.dot(active, w_down[0], preferred_element_type=jnp.float32).astype(jnp.bfloat16)
    outs = (outs.astype(jnp.float32) * slot_weight.reshape(-1, 1)).astype(jnp.bfloat16)
    part = jnp.einsum(
        "gct,gcd->gtd",
        pick,
        outs.reshape(groups, group_cap, D),
        preferred_element_type=jnp.float32,
    ).astype(jnp.bfloat16)
    return reduce_rows(part.reshape(blocks, tokens_dev, D), depth).astype(jnp.float32)


def shards(
    residual,
    queries,
    keys_values,
    out_grad,
    w_out,
    norm_gain,
    w_router,
    expert_ids,
    w_gate_up,
    w_down,
):
    tokens_dev = queries.shape[1]
    row_count = tokens_dev * HQ
    factor = HD ** (-0.5)
    head_rows = queries.reshape(row_count, HD)
    grad_rows = out_grad.reshape(row_count, HD)
    whole_pairs = lax.all_gather(keys_values, "ctx", axis=1, tiled=True)
    length = whole_pairs.shape[1]
    key_rows = whole_pairs[0, :, :HD]
    value_rows = whole_pairs[0, :, HD:]
    offset = lax.axis_index("ctx") * tokens_dev
    query_pos = offset + jnp.arange(row_count, dtype=jnp.int32) // HQ
    key_pos = jnp.arange(length, dtype=jnp.int32)
    causal = key_pos[None, :] <= query_pos[:, None]
    scores = (
        jnp.einsum("rd,kd->rk", head_rows, key_rows, preferred_element_type=jnp.float32) * factor
    )
    scores = jnp.where(causal, scores, -jnp.inf)
    highest = jnp.max(scores, axis=1, keepdims=True)
    weights = jnp.exp(scores - highest)
    totals = jnp.sum(weights, axis=1, keepdims=True)
    attn_probs = weights / totals
    probs_low = attn_probs.astype(jnp.bfloat16)
    attended = jnp.dot(probs_low, value_rows, preferred_element_type=jnp.float32).astype(
        jnp.bfloat16
    )
    row_dot = jnp.sum(
        grad_rows.astype(jnp.float32) * attended.astype(jnp.float32), axis=1, keepdims=True
    )
    prob_grad = jnp.einsum("rd,kd->rk", grad_rows, value_rows, preferred_element_type=jnp.float32)
    score_grad = (attn_probs * (prob_grad - row_dot)).astype(jnp.bfloat16)
    query_grad = (
        jnp.dot(score_grad, key_rows, preferred_element_type=jnp.float32) * factor
    ).astype(jnp.bfloat16)
    key_part = (
        jnp.einsum("rk,rd->kd", score_grad, head_rows, preferred_element_type=jnp.float32) * factor
    )
    value_part = jnp.einsum("rk,rd->kd", probs_low, grad_rows, preferred_element_type=jnp.float32)
    pair_grad = lax.psum_scatter(
        jnp.concatenate([key_part, value_part], axis=1).astype(jnp.bfloat16),
        "ctx",
        scatter_dimension=0,
        tiled=True,
    ).astype(jnp.float32)
    hidden = residual.reshape(tokens_dev, D).astype(jnp.float32) + jnp.dot(
        attended.reshape(tokens_dev, HQ * HD), w_out, preferred_element_type=jnp.float32
    )
    normed = (
        hidden * lax.rsqrt(jnp.mean(hidden * hidden, axis=1, keepdims=True) + norm_eps) * norm_gain
    ).astype(jnp.bfloat16)
    logits = jnp.dot(normed, w_router, preferred_element_type=jnp.float32)
    experts_all = w_router.shape[1]
    routed = expert_ids.reshape(tokens_dev, TOPK)
    route_match = routed[:, :, None] == jnp.arange(experts_all, dtype=jnp.int32)[None, None, :]
    chosen = jnp.sum(jnp.where(route_match, logits[:, None, :], 0.0), axis=2)
    gate_values = jax.nn.sigmoid(chosen)
    mixing = gate_values / jnp.sum(gate_values, axis=1, keepdims=True)
    if experts_all <= 4 * TOPK and lax.axis_size("dp") == 4 and w_gate_up.shape[0] == 1:
        dense_mix = jnp.sum(jnp.where(route_match, mixing[:, :, None], 0.0), axis=1)
        mixture = gathered_mixture(normed, dense_mix, w_gate_up, w_down)
    else:
        mixture = exchange_mixture(normed, routed, mixing, route_match, w_gate_up, w_down)
    layer_out = (hidden + mixture).astype(jnp.bfloat16).reshape(1, tokens_dev, D)
    return (
        layer_out,
        query_grad.reshape(1, tokens_dev, HQ * HD),
        pair_grad.reshape(1, tokens_dev, 2 * HD),
    )


def solution(mesh):
    placed = (
        P("dp", "ctx", None),
        P("dp", "ctx", None),
        P("dp", "ctx", None),
        P("dp", "ctx", None),
        P(),
        P(),
        P(),
        P("dp", "ctx", None),
        P(("dp", "ctx"), None, None),
        P(("dp", "ctx"), None, None),
    )
    return jax.shard_map(
        shards,
        mesh=mesh,
        in_specs=placed,
        out_specs=(P("dp", "ctx", None), P("dp", "ctx", None), P("dp", "ctx", None)),
        check_vma=False,
    )
```

```python
import functools

import jax
import jax.numpy as jnp
from jax import lax
from jax.experimental import pallas as pl
from jax.experimental.pallas import tpu as pltpu
from jax.sharding import PartitionSpec as P

D = 4096
HD = 128
TOPK = 8
HQ = 4


norm_eps = 1e-06


def expert_block(arrived, w_gate_up, w_down):
    hidden_width = w_down.shape[1]
    gate_up = jnp.einsum("sjid,jdf->sjif", arrived, w_gate_up, preferred_element_type=jnp.float32)
    active = (jax.nn.silu(gate_up[..., :hidden_width]) * gate_up[..., hidden_width:]).astype(
        jnp.bfloat16
    )
    return jnp.einsum("sjif,jfd->sjid", active, w_down, preferred_element_type=jnp.float32).astype(
        jnp.bfloat16
    )


def exchange_mixture(normed, routed, mixing, route_match, w_gate_up, w_down):
    tokens_dev, experts_all = normed.shape[0], route_match.shape[2]
    capacity = tokens_dev * TOPK // experts_all + 2
    onehot = route_match.reshape(tokens_dev * TOPK, experts_all).astype(jnp.int32)
    before = jnp.cumsum(onehot, axis=0) - onehot
    ranked = jnp.sum(before * onehot, axis=1)
    slot_index = routed.reshape(-1) * capacity + ranked
    repeated = jnp.repeat(normed, TOPK, axis=0)
    outgoing = jnp.zeros((experts_all * capacity, D), jnp.bfloat16).at[slot_index].set(repeated)
    dp_size = lax.axis_size("dp")
    ctx_size = lax.axis_size("ctx")
    per_dev = w_gate_up.shape[0]
    returned = lax.all_to_all(
        expert_block(
            lax.all_to_all(
                outgoing.reshape(dp_size * ctx_size, per_dev, capacity, D),
                ("dp", "ctx"),
                split_axis=0,
                concat_axis=0,
                tiled=True,
            ),
            w_gate_up,
            w_down,
        ),
        ("dp", "ctx"),
        split_axis=0,
        concat_axis=0,
        tiled=True,
    )
    results = returned.reshape(experts_all * capacity, D)[slot_index]
    mixture = jnp.einsum(
        "tk,tkd->td", mixing, results.reshape(tokens_dev, TOPK, D).astype(jnp.float32)
    )
    return mixture


MESH = pl.DeviceIdType.MESH


class Place:
    def __init__(self, depth):
        self.depth = depth
        self.dp = lax.axis_index("dp")
        ctx = lax.axis_index("ctx")
        self.z, self.core = ctx // 2, ctx % 2
        x_flip = (self.dp // 2) * 2 + 1 - self.dp % 2
        y_flip = (self.dp + 2) % 4
        self.near_dp = x_flip * (1 - self.core) + y_flip * self.core
        self.far_dp = y_flip * (1 - self.core) + x_flip * self.core
        self.both_dp = 3 - self.dp
        self.near = (self.near_dp, ctx)
        self.far = (self.far_dp, ctx)
        self.other_core = (self.dp, self.z * 2 + 1 - self.core)
        self.up = (self.dp, ctx + 2)
        self.down = (self.dp, ctx - 2)
        self.has_up = self.z < depth - 1
        self.has_down = self.z > 0

    def block(self, dp, z, core=None):
        return (dp * self.depth + z) * 2 + (self.core if core is None else core)

    def greet(self):
        barrier = pltpu.get_barrier_semaphore()
        for target in (self.near, self.far, self.other_core):
            pl.semaphore_signal(barrier, inc=1, device_id=target, device_id_type=MESH)

        @pl.when(self.has_up)
        def _():
            pl.semaphore_signal(barrier, inc=1, device_id=self.up, device_id_type=MESH)

        @pl.when(self.has_down)
        def _():
            pl.semaphore_signal(barrier, inc=1, device_id=self.down, device_id_type=MESH)

        pl.semaphore_wait(
            barrier, 3 + self.has_up.astype(jnp.int32) + self.has_down.astype(jnp.int32)
        )


def experts_kernel(
    depth,
    rows_ref,
    pick_ref,
    spread_ref,
    weight_ref,
    w_gate_up_ref,
    w_down_ref,
    part_ref,
    all_ref,
    gate_up_buf,
    down_buf,
    plane_rows,
    arrived,
    active,
    own_sem,
    send_sem,
    recv_sem,
    load_sem,
    weight_sem,
):
    place = Place(depth)
    z = place.z
    targets = (place.near, place.far, place.other_core, place.up, place.down)
    NEAR, FAR, CORE, UP, DOWN = range(5)
    own = place.block(place.dp, z)

    def copy(kind, block, source=None):
        return pltpu.make_async_remote_copy(
            src_ref=all_ref.at[block] if source is None else source,
            dst_ref=all_ref.at[block],
            send_sem=send_sem.at[kind, block],
            recv_sem=recv_sem.at[block],
            device_id=targets[kind],
            device_id_type=MESH,
        )

    def along(distance):
        if distance == 0:
            return [(z, None, None)]
        return [(z - distance, z >= distance, UP), (z + distance, z + distance < depth, DOWN)]

    def run(condition, body):
        if condition is None:
            body()
        else:
            pl.when(condition)(body)

    own_copy = pltpu.make_async_copy(rows_ref, all_ref.at[own], own_sem)
    place.greet()
    own_copy.start()
    pl.when(place.has_up)(lambda: copy(UP, own, rows_ref).start())
    pl.when(place.has_down)(lambda: copy(DOWN, own, rows_ref).start())
    for kind in (FAR, NEAR, CORE):
        copy(kind, own, rows_ref).start()
    weight_copies = (
        pltpu.make_async_copy(w_gate_up_ref, gate_up_buf, weight_sem.at[0]),
        pltpu.make_async_copy(w_down_ref, down_buf, weight_sem.at[1]),
    )
    weight_copies[0].start()
    weight_copies[1].start()

    def from_line(distance):
        for source, condition, onward in along(distance):

            def body(source=source, onward=onward):
                block = place.block(place.dp, source)
                copy(onward, block).wait_recv()
                more = place.has_up if onward == UP else place.has_down
                pl.when(more)(lambda: copy(onward, block).start())
                for kind in (NEAR, FAR, CORE):
                    copy(kind, block).start()

            run(condition, body)

    def from_near(distance):
        for source, condition, _ in along(distance):

            def body(source=source):
                block = place.block(place.near_dp, source)
                copy(NEAR, block).wait_recv()
                for kind in (FAR, CORE):
                    copy(kind, block).start()

            run(condition, body)

    def from_far(distance):
        for source, condition, _ in along(distance):

            def body(source=source):
                for dp in (place.far_dp, place.both_dp):
                    block = place.block(dp, source)
                    copy(FAR, block).wait_recv()
                    copy(CORE, block).start()

            run(condition, body)

    tokens_dev = rows_ref.shape[0]
    width, hidden_width = w_gate_up_ref.shape[0], w_down_ref.shape[0]

    def plane_at(turn):
        outward = lambda at: jnp.where(turn <= at, at - turn, turn)
        return jnp.where(z < depth // 2, outward(z), depth - 1 - outward(depth - 1 - z))

    def compute(turn):
        plane = plane_at(turn)
        for dp in range(4):
            copy(CORE, place.block(dp, plane, 1 - place.core)).wait_recv()
        pieces = [
            (place.block(dp, plane, core), plane_rows.at[pl.ds((dp * 2 + core) * tokens_dev, tokens_dev)])
            for dp in range(4)
            for core in range(2)
        ]
        loads = [
            pltpu.make_async_copy(all_ref.at[block], piece, load_sem.at[i])
            for i, (block, piece) in enumerate(pieces)
        ]
        stores = [
            pltpu.make_async_copy(piece, part_ref.at[block], load_sem.at[i])
            for i, (block, piece) in enumerate(pieces)
        ]
        for load in loads:
            load.start()
        for load in loads:
            load.wait()

        def pick_columns(i, carry):
            at = pl.ds(pl.multiple_of(i * 512, 512), 512)
            arrived[:, at] = jnp.dot(
                pick_ref[plane], plane_rows[:, at], preferred_element_type=jnp.float32
            ).astype(jnp.bfloat16)
            return carry

        def up_columns(i, carry):
            at = pl.ds(pl.multiple_of(i * 256, 256), 256)
            up_at = pl.ds(pl.multiple_of(hidden_width + i * 256, 256), 256)
            gate = jnp.dot(arrived[...], gate_up_buf[:, at], preferred_element_type=jnp.float32)
            up = jnp.dot(arrived[...], gate_up_buf[:, up_at], preferred_element_type=jnp.float32)
            active[:, at] = (gate / (1.0 + jnp.exp(-gate)) * up).astype(jnp.bfloat16)
            return carry

        def down_columns(i, carry):
            at = pl.ds(pl.multiple_of(i * 512, 512), 512)
            out = jnp.dot(active[...], down_buf[:, at], preferred_element_type=jnp.float32)
            out = out.astype(jnp.bfloat16).astype(jnp.float32) * weight_ref[plane]
            plane_rows[:, at] = jnp.dot(
                spread_ref[plane], out.astype(jnp.bfloat16), preferred_element_type=jnp.float32
            ).astype(jnp.bfloat16)
            return carry

        lax.fori_loop(0, width // 512, pick_columns, 0)
        lax.fori_loop(0, hidden_width // 256, up_columns, 0)
        lax.fori_loop(0, width // 512, down_columns, 0)
        for store in stores:
            store.start()
        for store in stores:
            store.wait()

    for distance in range(depth):
        if distance:
            from_line(distance)
        from_near(distance)
        if distance:
            from_far(distance - 1)
            if distance == 1:
                own_copy.wait()
                weight_copies[0].wait()
                weight_copies[1].wait()
            compute(distance - 1)
    from_far(depth - 1)
    compute(depth - 1)
    for distance in range(depth):
        for source, condition, onward in along(distance):

            def body(source=source, onward=onward):
                block = place.block(place.dp, source)
                for kind in (NEAR, FAR, CORE):
                    copy(kind, block).wait_send()
                if onward != DOWN:
                    pl.when(place.has_up)(lambda: copy(UP, block).wait_send())
                if onward != UP:
                    pl.when(place.has_down)(lambda: copy(DOWN, block).wait_send())
                block = place.block(place.near_dp, source)
                for kind in (FAR, CORE):
                    copy(kind, block).wait_send()
                for dp in (place.far_dp, place.both_dp):
                    copy(CORE, place.block(dp, source)).wait_send()

            run(condition, body)


def gather_and_apply(rows, pick, spread, slot_weight, w_gate_up, w_down, depth):
    tokens_dev, width = rows.shape
    blocks = 8 * depth
    slots, plane_tokens = pick.shape[1:]
    gathered = jax.ShapeDtypeStruct((blocks, tokens_dev, width), rows.dtype)
    anywhere = pl.BlockSpec(memory_space=pl.ANY)
    in_vmem = pl.BlockSpec(memory_space=pltpu.VMEM)
    part, _ = pl.pallas_call(
        functools.partial(experts_kernel, depth),
        out_shape=(gathered, gathered),
        in_specs=[anywhere, in_vmem, in_vmem, in_vmem, anywhere, anywhere],
        out_specs=(anywhere, anywhere),
        scratch_shapes=[
            pltpu.VMEM(w_gate_up.shape, w_gate_up.dtype),
            pltpu.VMEM(w_down.shape, w_down.dtype),
            pltpu.VMEM((plane_tokens, width), rows.dtype),
            pltpu.VMEM((slots, width), rows.dtype),
            pltpu.VMEM((slots, w_down.shape[0]), rows.dtype),
            pltpu.SemaphoreType.DMA(()),
            pltpu.SemaphoreType.DMA((5, blocks)),
            pltpu.SemaphoreType.DMA((blocks,)),
            pltpu.SemaphoreType.DMA((8,)),
            pltpu.SemaphoreType.DMA((2,)),
        ],
        compiler_params=pltpu.CompilerParams(
            collective_id=1, has_side_effects=True, vmem_limit_bytes=58 * 2**20
        ),
    )(rows, pick, spread, slot_weight, w_gate_up, w_down)
    return part


def reduce_kernel(
    depth,
    part_ref,
    out_ref,
    total,
    core_in,
    far_in,
    near_in,
    line_in,
    own_sem,
    core_send,
    core_recv,
    far_send,
    far_recv,
    near_send,
    near_recv,
    line_send,
    line_recv,
):
    place = Place(depth)
    z = place.z
    rows = out_ref.shape[0]

    def order(i):
        falling = lambda at: jnp.where(
            depth - 1 - i > at, depth - 1 - i, depth - 2 - i if i < depth - 1 else at
        )
        return jnp.where(z < depth // 2, falling(z), depth - 1 - falling(depth - 1 - z))

    levels = [order(i) for i in range(depth)]

    def add(into, term):
        def step(i, carry):
            at = pl.ds(pl.multiple_of(i * 16, 16), 16)
            into[at, :] = (
                into[at, :].astype(jnp.float32) + term[at, :].astype(jnp.float32)
            ).astype(jnp.bfloat16)
            return carry

        lax.fori_loop(0, rows // 16, step, 0)

    def remote(source, into, send, recv, target):
        return pltpu.make_async_remote_copy(
            src_ref=source,
            dst_ref=into,
            send_sem=send,
            recv_sem=recv,
            device_id=target,
            device_id_type=MESH,
        )

    def slot(dp, level):
        return dp * depth + level

    def load(dp, level):
        at = slot(dp, level)
        return pltpu.make_async_copy(
            part_ref.at[place.block(dp, level)], total.at[at], own_sem.at[at]
        )

    def to_core(dp, level):
        at = slot(dp, level)
        return remote(
            part_ref.at[place.block(dp, level, 1 - place.core)],
            core_in.at[at],
            core_send.at[at],
            core_recv.at[at],
            place.other_core,
        )

    def to_far(side, dp, level):
        at = side * depth + level
        return remote(
            total.at[slot(dp, level)], far_in.at[at], far_send.at[at], far_recv.at[at], place.far
        )

    def to_near(level):
        return remote(
            total.at[slot(place.near_dp, level)],
            near_in.at[level],
            near_send.at[level],
            near_recv.at[level],
            place.near,
        )

    def to_line(level, at, target):
        return remote(
            total.at[slot(place.dp, level)],
            line_in.at[at],
            line_send.at[level],
            line_recv.at[at],
            target,
        )

    place.greet()
    theirs = (place.both_dp, place.near_dp, place.far_dp, place.dp)
    mine = (place.both_dp, place.far_dp, place.near_dp, place.dp)
    for dp in range(4):
        for level in levels:
            to_core(theirs[dp], level).start()
            load(mine[dp], level).start()
    for turn, dp in enumerate(mine):
        for level in levels:
            at = slot(dp, level)
            load(dp, level).wait()
            to_core(dp, level).wait_recv()
            add(total.at[at], core_in.at[at])
            if turn < 2:
                to_far(1 - turn, dp, level).start()
    for level in levels:
        at = slot(place.near_dp, level)
        to_far(1, place.both_dp, level).wait_recv()
        add(total.at[at], far_in.at[depth + level])
        to_near(level).start()
    for level in levels:
        at = slot(place.dp, level)
        to_far(0, place.far_dp, level).wait_recv()
        add(total.at[at], far_in.at[level])
        to_near(level).wait_recv()
        add(total.at[at], near_in.at[level])

        @pl.when(level > z)
        def _():
            @pl.when(place.has_down)
            def _():
                to_line(level, level, place.up).wait_recv()
                add(total.at[at], line_in.at[level])

            to_line(level, level, place.up).start()

        @pl.when(level < z)
        def _():
            @pl.when(place.has_up)
            def _():
                to_line(level, level, place.down).wait_recv()
                add(total.at[at], line_in.at[level])

            to_line(level, jnp.where(level == z - 1, depth, level), place.down).start()

    at = slot(place.dp, z)

    @pl.when(place.has_down)
    def _():
        to_line(z, z, place.up).wait_recv()
        add(total.at[at], line_in.at[z])

    @pl.when(place.has_up)
    def _():
        to_line(z, depth, place.down).wait_recv()
        add(total.at[at], line_in.at[depth])

    out_ref[...] = total[at]

    for dp in range(4):
        for level in levels:
            to_core(theirs[dp], level).wait_send()
    for level in levels:
        to_far(1, place.both_dp, level).wait_send()
        to_far(0, place.far_dp, level).wait_send()
        to_near(level).wait_send()

        @pl.when(level != z)
        def _():
            to_line(level, level, place.up).wait_send()


def reduce_rows(part, depth):
    blocks, tokens_dev, width = part.shape
    half = blocks // 2

    def buffer(count):
        return pltpu.VMEM((count, tokens_dev, width), part.dtype)

    def sems(count):
        return pltpu.SemaphoreType.DMA((count,))

    return pl.pallas_call(
        functools.partial(reduce_kernel, depth),
        out_shape=jax.ShapeDtypeStruct((tokens_dev, width), part.dtype),
        in_specs=[pl.BlockSpec(memory_space=pl.ANY)],
        out_specs=pl.BlockSpec(memory_space=pltpu.VMEM),
        scratch_shapes=[
            buffer(half),
            buffer(half),
            buffer(2 * depth),
            buffer(depth),
            buffer(depth + 1),
            sems(half),
            sems(half),
            sems(half),
            sems(2 * depth),
            sems(2 * depth),
            sems(depth),
            sems(depth),
            sems(depth),
            sems(depth + 1),
        ],
        compiler_params=pltpu.CompilerParams(
            collective_id=2, has_side_effects=True, vmem_limit_bytes=60 * 2**20
        ),
    )(part)


def gathered_mixture(normed, dense_mix, w_gate_up, w_down):
    tokens_dev, experts_all = dense_mix.shape
    axes = ("dp", "ctx")
    depth = lax.axis_size("ctx") // 2
    capacity = tokens_dev * TOPK // experts_all + 2
    slot_count, plane_tokens = 8 * capacity, 8 * tokens_dev
    weights = lax.all_to_all(
        dense_mix.T.reshape(experts_all, 1, tokens_dev), axes, split_axis=0, concat_axis=0, tiled=True
    )
    weights = (
        weights.reshape(4, depth, 2, tokens_dev).transpose(1, 0, 2, 3).reshape(depth, plane_tokens)
    )
    named = weights != 0.0
    rank = jnp.cumsum(named.astype(jnp.int32), axis=1) - 1
    slots = jnp.arange(slot_count, dtype=jnp.int32)
    pick = (rank[:, None, :] == slots[None, :, None]) & named[:, None, :]
    slot_weight = jnp.sum(jnp.where(pick, weights[:, None, :], 0.0), axis=2, keepdims=True)
    spread = (rank[:, :, None] == slots[None, None, :]) & named[:, :, None]
    part = gather_and_apply(
        normed,
        pick.astype(jnp.bfloat16),
        spread.astype(jnp.bfloat16),
        slot_weight,
        w_gate_up[0],
        w_down[0],
        depth,
    )
    return reduce_rows(part, depth).astype(jnp.float32)


def shards(
    residual,
    queries,
    keys_values,
    out_grad,
    w_out,
    norm_gain,
    w_router,
    expert_ids,
    w_gate_up,
    w_down,
):
    tokens_dev = queries.shape[1]
    row_count = tokens_dev * HQ
    factor = HD ** (-0.5)
    head_rows = queries.reshape(row_count, HD)
    grad_rows = out_grad.reshape(row_count, HD)
    whole_pairs = lax.all_gather(keys_values, "ctx", axis=1, tiled=True)
    length = whole_pairs.shape[1]
    key_rows = whole_pairs[0, :, :HD]
    value_rows = whole_pairs[0, :, HD:]
    offset = lax.axis_index("ctx") * tokens_dev
    query_pos = offset + jnp.arange(row_count, dtype=jnp.int32) // HQ
    key_pos = jnp.arange(length, dtype=jnp.int32)
    causal = key_pos[None, :] <= query_pos[:, None]
    scores = (
        jnp.einsum("rd,kd->rk", head_rows, key_rows, preferred_element_type=jnp.float32) * factor
    )
    scores = jnp.where(causal, scores, -jnp.inf)
    highest = jnp.max(scores, axis=1, keepdims=True)
    weights = jnp.exp(scores - highest)
    totals = jnp.sum(weights, axis=1, keepdims=True)
    attn_probs = weights / totals
    probs_low = attn_probs.astype(jnp.bfloat16)
    attended = jnp.dot(probs_low, value_rows, preferred_element_type=jnp.float32).astype(
        jnp.bfloat16
    )
    row_dot = jnp.sum(
        grad_rows.astype(jnp.float32) * attended.astype(jnp.float32), axis=1, keepdims=True
    )
    prob_grad = jnp.einsum("rd,kd->rk", grad_rows, value_rows, preferred_element_type=jnp.float32)
    score_grad = (attn_probs * (prob_grad - row_dot)).astype(jnp.bfloat16)
    query_grad = (
        jnp.dot(score_grad, key_rows, preferred_element_type=jnp.float32) * factor
    ).astype(jnp.bfloat16)
    key_part = (
        jnp.einsum("rk,rd->kd", score_grad, head_rows, preferred_element_type=jnp.float32) * factor
    )
    value_part = jnp.einsum("rk,rd->kd", probs_low, grad_rows, preferred_element_type=jnp.float32)
    pair_grad = lax.psum_scatter(
        jnp.concatenate([key_part, value_part], axis=1).astype(jnp.bfloat16),
        "ctx",
        scatter_dimension=0,
        tiled=True,
    ).astype(jnp.float32)
    hidden = residual.reshape(tokens_dev, D).astype(jnp.float32) + jnp.dot(
        attended.reshape(tokens_dev, HQ * HD), w_out, preferred_element_type=jnp.float32
    )
    normed = (
        hidden * lax.rsqrt(jnp.mean(hidden * hidden, axis=1, keepdims=True) + norm_eps) * norm_gain
    ).astype(jnp.bfloat16)
    logits = jnp.dot(normed, w_router, preferred_element_type=jnp.float32)
    experts_all = w_router.shape[1]
    routed = expert_ids.reshape(tokens_dev, TOPK)
    route_match = routed[:, :, None] == jnp.arange(experts_all, dtype=jnp.int32)[None, None, :]
    chosen = jnp.sum(jnp.where(route_match, logits[:, None, :], 0.0), axis=2)
    gate_values = jax.nn.sigmoid(chosen)
    mixing = gate_values / jnp.sum(gate_values, axis=1, keepdims=True)
    if experts_all <= 4 * TOPK and lax.axis_size("dp") == 4 and w_gate_up.shape[0] == 1:
        dense_mix = jnp.sum(jnp.where(route_match, mixing[:, :, None], 0.0), axis=1)
        mixture = gathered_mixture(normed, dense_mix, w_gate_up, w_down)
    else:
        mixture = exchange_mixture(normed, routed, mixing, route_match, w_gate_up, w_down)
    layer_out = (hidden + mixture).astype(jnp.bfloat16).reshape(1, tokens_dev, D)
    return (
        layer_out,
        query_grad.reshape(1, tokens_dev, HQ * HD),
        pair_grad.reshape(1, tokens_dev, 2 * HD),
    )


def solution(mesh):
    placed = (
        P("dp", "ctx", None),
        P("dp", "ctx", None),
        P("dp", "ctx", None),
        P("dp", "ctx", None),
        P(),
        P(),
        P(),
        P("dp", "ctx", None),
        P(("dp", "ctx"), None, None),
        P(("dp", "ctx"), None, None),
    )
    return jax.shard_map(
        shards,
        mesh=mesh,
        in_specs=placed,
        out_specs=(P("dp", "ctx", None), P("dp", "ctx", None), P("dp", "ctx", None)),
        check_vma=False,
    )
```

```python
import functools

import jax
import jax.numpy as jnp
from jax import lax
from jax.experimental import pallas as pl
from jax.experimental.pallas import tpu as pltpu
from jax.sharding import PartitionSpec as P

D = 4096
HD = 128
TOPK = 8
HQ = 4


norm_eps = 1e-06


def expert_block(arrived, w_gate_up, w_down):
    hidden_width = w_down.shape[1]
    gate_up = jnp.einsum("sjid,jdf->sjif", arrived, w_gate_up, preferred_element_type=jnp.float32)
    active = (jax.nn.silu(gate_up[..., :hidden_width]) * gate_up[..., hidden_width:]).astype(
        jnp.bfloat16
    )
    return jnp.einsum("sjif,jfd->sjid", active, w_down, preferred_element_type=jnp.float32).astype(
        jnp.bfloat16
    )


def exchange_mixture(normed, routed, mixing, route_match, w_gate_up, w_down):
    tokens_dev, experts_all = normed.shape[0], route_match.shape[2]
    capacity = tokens_dev * TOPK // experts_all + 2
    onehot = route_match.reshape(tokens_dev * TOPK, experts_all).astype(jnp.int32)
    before = jnp.cumsum(onehot, axis=0) - onehot
    ranked = jnp.sum(before * onehot, axis=1)
    slot_index = routed.reshape(-1) * capacity + ranked
    repeated = jnp.repeat(normed, TOPK, axis=0)
    outgoing = jnp.zeros((experts_all * capacity, D), jnp.bfloat16).at[slot_index].set(repeated)
    dp_size = lax.axis_size("dp")
    ctx_size = lax.axis_size("ctx")
    per_dev = w_gate_up.shape[0]
    returned = lax.all_to_all(
        expert_block(
            lax.all_to_all(
                outgoing.reshape(dp_size * ctx_size, per_dev, capacity, D),
                ("dp", "ctx"),
                split_axis=0,
                concat_axis=0,
                tiled=True,
            ),
            w_gate_up,
            w_down,
        ),
        ("dp", "ctx"),
        split_axis=0,
        concat_axis=0,
        tiled=True,
    )
    results = returned.reshape(experts_all * capacity, D)[slot_index]
    mixture = jnp.einsum(
        "tk,tkd->td", mixing, results.reshape(tokens_dev, TOPK, D).astype(jnp.float32)
    )
    return mixture


MESH = pl.DeviceIdType.MESH


class Place:
    def __init__(self, depth):
        self.depth = depth
        self.dp = lax.axis_index("dp")
        ctx = lax.axis_index("ctx")
        self.z, self.core = ctx // 2, ctx % 2
        x_flip = (self.dp // 2) * 2 + 1 - self.dp % 2
        y_flip = (self.dp + 2) % 4
        self.near_dp = x_flip * (1 - self.core) + y_flip * self.core
        self.far_dp = y_flip * (1 - self.core) + x_flip * self.core
        self.both_dp = 3 - self.dp
        self.near = (self.near_dp, ctx)
        self.far = (self.far_dp, ctx)
        self.other_core = (self.dp, self.z * 2 + 1 - self.core)
        self.up = (self.dp, ctx + 2)
        self.down = (self.dp, ctx - 2)
        self.has_up = self.z < depth - 1
        self.has_down = self.z > 0

    def block(self, dp, z, core=None):
        return (dp * self.depth + z) * 2 + (self.core if core is None else core)

    def greet(self):
        barrier = pltpu.get_barrier_semaphore()
        for target in (self.near, self.far, self.other_core):
            pl.semaphore_signal(barrier, inc=1, device_id=target, device_id_type=MESH)

        @pl.when(self.has_up)
        def _():
            pl.semaphore_signal(barrier, inc=1, device_id=self.up, device_id_type=MESH)

        @pl.when(self.has_down)
        def _():
            pl.semaphore_signal(barrier, inc=1, device_id=self.down, device_id_type=MESH)

        pl.semaphore_wait(
            barrier, 3 + self.has_up.astype(jnp.int32) + self.has_down.astype(jnp.int32)
        )


def experts_kernel(
    depth,
    rows_ref,
    pick_ref,
    spread_ref,
    weight_ref,
    w_gate_up_ref,
    w_down_ref,
    part_ref,
    all_ref,
    gate_up_buf,
    down_buf,
    plane_rows,
    arrived,
    active,
    own_sem,
    send_sem,
    recv_sem,
    load_sem,
    weight_sem,
):
    place = Place(depth)
    z = place.z
    targets = (place.near, place.far, place.other_core, place.up, place.down)
    NEAR, FAR, CORE, UP, DOWN = range(5)
    own = place.block(place.dp, z)

    def copy(kind, block, source=None):
        return pltpu.make_async_remote_copy(
            src_ref=all_ref.at[block] if source is None else source,
            dst_ref=all_ref.at[block],
            send_sem=send_sem.at[kind, block],
            recv_sem=recv_sem.at[block],
            device_id=targets[kind],
            device_id_type=MESH,
        )

    def along(distance):
        if distance == 0:
            return [(z, None, None)]
        return [(z - distance, z >= distance, UP), (z + distance, z + distance < depth, DOWN)]

    def run(condition, body):
        if condition is None:
            body()
        else:
            pl.when(condition)(body)

    own_copy = pltpu.make_async_copy(rows_ref, all_ref.at[own], own_sem)
    place.greet()
    own_copy.start()
    pl.when(place.has_up)(lambda: copy(UP, own, rows_ref).start())
    pl.when(place.has_down)(lambda: copy(DOWN, own, rows_ref).start())
    for kind in (FAR, NEAR, CORE):
        copy(kind, own, rows_ref).start()
    weight_copies = (
        pltpu.make_async_copy(w_gate_up_ref, gate_up_buf, weight_sem.at[0]),
        pltpu.make_async_copy(w_down_ref, down_buf, weight_sem.at[1]),
    )
    weight_copies[0].start()
    weight_copies[1].start()

    def from_line(distance):
        for source, condition, onward in along(distance):

            def body(source=source, onward=onward):
                block = place.block(place.dp, source)
                copy(onward, block).wait_recv()
                more = place.has_up if onward == UP else place.has_down
                pl.when(more)(lambda: copy(onward, block).start())
                for kind in (NEAR, FAR, CORE):
                    copy(kind, block).start()

            run(condition, body)

    def from_near(distance):
        for source, condition, _ in along(distance):

            def body(source=source):
                block = place.block(place.near_dp, source)
                copy(NEAR, block).wait_recv()
                for kind in (FAR, CORE):
                    copy(kind, block).start()

            run(condition, body)

    def from_far(distance):
        for source, condition, _ in along(distance):

            def body(source=source):
                for dp in (place.far_dp, place.both_dp):
                    block = place.block(dp, source)
                    copy(FAR, block).wait_recv()
                    copy(CORE, block).start()

            run(condition, body)

    tokens_dev = rows_ref.shape[0]
    width, hidden_width = w_gate_up_ref.shape[0], w_down_ref.shape[0]

    def plane_at(turn):
        outward = lambda at: jnp.where(turn <= at, at - turn, turn)
        return jnp.where(z < depth // 2, outward(z), depth - 1 - outward(depth - 1 - z))

    def compute(turn):
        plane = plane_at(turn)
        for dp in range(4):
            copy(CORE, place.block(dp, plane, 1 - place.core)).wait_recv()
        pieces = [
            (place.block(dp, plane, core), plane_rows.at[pl.ds((dp * 2 + core) * tokens_dev, tokens_dev)])
            for dp in range(4)
            for core in range(2)
        ]
        loads = [
            pltpu.make_async_copy(all_ref.at[block], piece, load_sem.at[i])
            for i, (block, piece) in enumerate(pieces)
        ]
        stores = [
            pltpu.make_async_copy(piece, part_ref.at[block], load_sem.at[i])
            for i, (block, piece) in enumerate(pieces)
        ]
        for load in loads:
            load.start()
        for load in loads:
            load.wait()

        def pick_columns(i, carry):
            at = pl.ds(pl.multiple_of(i * 512, 512), 512)
            arrived[:, at] = jnp.dot(
                pick_ref[plane], plane_rows[:, at], preferred_element_type=jnp.float32
            ).astype(jnp.bfloat16)
            return carry

        def up_columns(i, carry):
            at = pl.ds(pl.multiple_of(i * 256, 256), 256)
            up_at = pl.ds(pl.multiple_of(hidden_width + i * 256, 256), 256)
            gate = jnp.dot(arrived[...], gate_up_buf[:, at], preferred_element_type=jnp.float32)
            up = jnp.dot(arrived[...], gate_up_buf[:, up_at], preferred_element_type=jnp.float32)
            active[:, at] = (gate / (1.0 + jnp.exp(-gate)) * up).astype(jnp.bfloat16)
            return carry

        def down_columns(i, carry):
            at = pl.ds(pl.multiple_of(i * 512, 512), 512)
            out = jnp.dot(active[...], down_buf[:, at], preferred_element_type=jnp.float32)
            out = out.astype(jnp.bfloat16).astype(jnp.float32) * weight_ref[plane]
            plane_rows[:, at] = jnp.dot(
                spread_ref[plane], out.astype(jnp.bfloat16), preferred_element_type=jnp.float32
            ).astype(jnp.bfloat16)
            return carry

        lax.fori_loop(0, width // 512, pick_columns, 0)
        lax.fori_loop(0, hidden_width // 256, up_columns, 0)
        lax.fori_loop(0, width // 512, down_columns, 0)
        for store in stores:
            store.start()
        for store in stores:
            store.wait()

    for distance in range(depth):
        if distance:
            from_line(distance)
        from_near(distance)
        if distance > 1:
            from_far(distance - 2)
    own_copy.wait()
    weight_copies[0].wait()
    weight_copies[1].wait()
    for turn in range(depth):
        if turn >= depth - 2:
            from_far(turn)
        compute(turn)
    for distance in range(depth):
        for source, condition, onward in along(distance):

            def body(source=source, onward=onward):
                block = place.block(place.dp, source)
                for kind in (NEAR, FAR, CORE):
                    copy(kind, block).wait_send()
                if onward != DOWN:
                    pl.when(place.has_up)(lambda: copy(UP, block).wait_send())
                if onward != UP:
                    pl.when(place.has_down)(lambda: copy(DOWN, block).wait_send())
                block = place.block(place.near_dp, source)
                for kind in (FAR, CORE):
                    copy(kind, block).wait_send()
                for dp in (place.far_dp, place.both_dp):
                    copy(CORE, place.block(dp, source)).wait_send()

            run(condition, body)


def gather_and_apply(rows, pick, spread, slot_weight, w_gate_up, w_down, depth):
    tokens_dev, width = rows.shape
    blocks = 8 * depth
    slots, plane_tokens = pick.shape[1:]
    gathered = jax.ShapeDtypeStruct((blocks, tokens_dev, width), rows.dtype)
    anywhere = pl.BlockSpec(memory_space=pl.ANY)
    in_vmem = pl.BlockSpec(memory_space=pltpu.VMEM)
    part, _ = pl.pallas_call(
        functools.partial(experts_kernel, depth),
        out_shape=(gathered, gathered),
        in_specs=[anywhere, in_vmem, in_vmem, in_vmem, anywhere, anywhere],
        out_specs=(anywhere, anywhere),
        scratch_shapes=[
            pltpu.VMEM(w_gate_up.shape, w_gate_up.dtype),
            pltpu.VMEM(w_down.shape, w_down.dtype),
            pltpu.VMEM((plane_tokens, width), rows.dtype),
            pltpu.VMEM((slots, width), rows.dtype),
            pltpu.VMEM((slots, w_down.shape[0]), rows.dtype),
            pltpu.SemaphoreType.DMA(()),
            pltpu.SemaphoreType.DMA((5, blocks)),
            pltpu.SemaphoreType.DMA((blocks,)),
            pltpu.SemaphoreType.DMA((8,)),
            pltpu.SemaphoreType.DMA((2,)),
        ],
        compiler_params=pltpu.CompilerParams(
            collective_id=1, has_side_effects=True, vmem_limit_bytes=58 * 2**20
        ),
    )(rows, pick, spread, slot_weight, w_gate_up, w_down)
    return part


def reduce_kernel(
    depth,
    part_ref,
    out_ref,
    total,
    core_in,
    far_in,
    near_in,
    line_in,
    own_sem,
    core_send,
    core_recv,
    far_send,
    far_recv,
    near_send,
    near_recv,
    line_send,
    line_recv,
):
    place = Place(depth)
    z = place.z
    rows = out_ref.shape[0]

    def order(i):
        falling = lambda at: jnp.where(
            depth - 1 - i > at, depth - 1 - i, depth - 2 - i if i < depth - 1 else at
        )
        return jnp.where(z < depth // 2, falling(z), depth - 1 - falling(depth - 1 - z))

    levels = [order(i) for i in range(depth)]

    def add(into, term):
        def step(i, carry):
            at = pl.ds(pl.multiple_of(i * 16, 16), 16)
            into[at, :] = (
                into[at, :].astype(jnp.float32) + term[at, :].astype(jnp.float32)
            ).astype(jnp.bfloat16)
            return carry

        lax.fori_loop(0, rows // 16, step, 0)

    def remote(source, into, send, recv, target):
        return pltpu.make_async_remote_copy(
            src_ref=source,
            dst_ref=into,
            send_sem=send,
            recv_sem=recv,
            device_id=target,
            device_id_type=MESH,
        )

    def slot(dp, level):
        return dp * depth + level

    def load(dp, level):
        at = slot(dp, level)
        return pltpu.make_async_copy(
            part_ref.at[place.block(dp, level)], total.at[at], own_sem.at[at]
        )

    def to_core(dp, level):
        at = slot(dp, level)
        return remote(
            part_ref.at[place.block(dp, level, 1 - place.core)],
            core_in.at[at],
            core_send.at[at],
            core_recv.at[at],
            place.other_core,
        )

    def to_far(side, dp, level):
        at = side * depth + level
        return remote(
            total.at[slot(dp, level)], far_in.at[at], far_send.at[at], far_recv.at[at], place.far
        )

    def to_near(level):
        return remote(
            total.at[slot(place.near_dp, level)],
            near_in.at[level],
            near_send.at[level],
            near_recv.at[level],
            place.near,
        )

    def to_line(level, at, target):
        return remote(
            total.at[slot(place.dp, level)],
            line_in.at[at],
            line_send.at[level],
            line_recv.at[at],
            target,
        )

    place.greet()
    theirs = (place.both_dp, place.near_dp, place.far_dp, place.dp)
    mine = (place.both_dp, place.far_dp, place.near_dp, place.dp)
    for half in ((0, 1), (2, 3)):
        for level in levels:
            for turn in half:
                to_core(theirs[turn], level).start()
                load(mine[turn], level).start()
    for half in ((0, 1), (2, 3)):
        for level in levels:
            for turn in half:
                at = slot(mine[turn], level)
                load(mine[turn], level).wait()
                to_core(mine[turn], level).wait_recv()
                add(total.at[at], core_in.at[at])
                if turn < 2:
                    to_far(1 - turn, mine[turn], level).start()

    def pass_near(level):
        at = slot(place.near_dp, level)
        to_far(1, place.both_dp, level).wait_recv()
        add(total.at[at], far_in.at[depth + level])
        to_near(level).start()

    pass_near(levels[0])
    for i, level in enumerate(levels):
        if i + 1 < depth:
            pass_near(levels[i + 1])
        at = slot(place.dp, level)
        to_far(0, place.far_dp, level).wait_recv()
        add(total.at[at], far_in.at[level])
        to_near(level).wait_recv()
        add(total.at[at], near_in.at[level])

        @pl.when(level > z)
        def _():
            @pl.when(place.has_down)
            def _():
                to_line(level, level, place.up).wait_recv()
                add(total.at[at], line_in.at[level])

            to_line(level, level, place.up).start()

        @pl.when(level < z)
        def _():
            @pl.when(place.has_up)
            def _():
                to_line(level, level, place.down).wait_recv()
                add(total.at[at], line_in.at[level])

            to_line(level, jnp.where(level == z - 1, depth, level), place.down).start()

    at = slot(place.dp, z)

    @pl.when(place.has_down)
    def _():
        to_line(z, z, place.up).wait_recv()
        add(total.at[at], line_in.at[z])

    @pl.when(place.has_up)
    def _():
        to_line(z, depth, place.down).wait_recv()
        add(total.at[at], line_in.at[depth])

    out_ref[...] = total[at]

    for dp in range(4):
        for level in levels:
            to_core(theirs[dp], level).wait_send()
    for level in levels:
        to_far(1, place.both_dp, level).wait_send()
        to_far(0, place.far_dp, level).wait_send()
        to_near(level).wait_send()

        @pl.when(level != z)
        def _():
            to_line(level, level, place.up).wait_send()


def reduce_rows(part, depth):
    blocks, tokens_dev, width = part.shape
    half = blocks // 2

    def buffer(count):
        return pltpu.VMEM((count, tokens_dev, width), part.dtype)

    def sems(count):
        return pltpu.SemaphoreType.DMA((count,))

    return pl.pallas_call(
        functools.partial(reduce_kernel, depth),
        out_shape=jax.ShapeDtypeStruct((tokens_dev, width), part.dtype),
        in_specs=[pl.BlockSpec(memory_space=pl.ANY)],
        out_specs=pl.BlockSpec(memory_space=pltpu.VMEM),
        scratch_shapes=[
            buffer(half),
            buffer(half),
            buffer(2 * depth),
            buffer(depth),
            buffer(depth + 1),
            sems(half),
            sems(half),
            sems(half),
            sems(2 * depth),
            sems(2 * depth),
            sems(depth),
            sems(depth),
            sems(depth),
            sems(depth + 1),
        ],
        compiler_params=pltpu.CompilerParams(
            collective_id=2, has_side_effects=True, vmem_limit_bytes=60 * 2**20
        ),
    )(part)


def gathered_mixture(normed, dense_mix, w_gate_up, w_down):
    tokens_dev, experts_all = dense_mix.shape
    axes = ("dp", "ctx")
    depth = lax.axis_size("ctx") // 2
    capacity = tokens_dev * TOPK // experts_all + 2
    slot_count, plane_tokens = 8 * capacity, 8 * tokens_dev
    weights = lax.all_to_all(
        dense_mix.T.reshape(experts_all, 1, tokens_dev), axes, split_axis=0, concat_axis=0, tiled=True
    )
    weights = (
        weights.reshape(4, depth, 2, tokens_dev).transpose(1, 0, 2, 3).reshape(depth, plane_tokens)
    )
    named = weights != 0.0
    rank = jnp.cumsum(named.astype(jnp.int32), axis=1) - 1
    slots = jnp.arange(slot_count, dtype=jnp.int32)
    pick = (rank[:, None, :] == slots[None, :, None]) & named[:, None, :]
    slot_weight = jnp.sum(jnp.where(pick, weights[:, None, :], 0.0), axis=2, keepdims=True)
    spread = (rank[:, :, None] == slots[None, None, :]) & named[:, :, None]
    part = gather_and_apply(
        normed,
        pick.astype(jnp.bfloat16),
        spread.astype(jnp.bfloat16),
        slot_weight,
        w_gate_up[0],
        w_down[0],
        depth,
    )
    return reduce_rows(part, depth).astype(jnp.float32)


def shards(
    residual,
    queries,
    keys_values,
    out_grad,
    w_out,
    norm_gain,
    w_router,
    expert_ids,
    w_gate_up,
    w_down,
):
    tokens_dev = queries.shape[1]
    row_count = tokens_dev * HQ
    factor = HD ** (-0.5)
    head_rows = queries.reshape(row_count, HD)
    grad_rows = out_grad.reshape(row_count, HD)
    whole_pairs = lax.all_gather(keys_values, "ctx", axis=1, tiled=True)
    length = whole_pairs.shape[1]
    key_rows = whole_pairs[0, :, :HD]
    value_rows = whole_pairs[0, :, HD:]
    offset = lax.axis_index("ctx") * tokens_dev
    query_pos = offset + jnp.arange(row_count, dtype=jnp.int32) // HQ
    key_pos = jnp.arange(length, dtype=jnp.int32)
    causal = key_pos[None, :] <= query_pos[:, None]
    scores = (
        jnp.einsum("rd,kd->rk", head_rows, key_rows, preferred_element_type=jnp.float32) * factor
    )
    scores = jnp.where(causal, scores, -jnp.inf)
    highest = jnp.max(scores, axis=1, keepdims=True)
    weights = jnp.exp(scores - highest)
    totals = jnp.sum(weights, axis=1, keepdims=True)
    attn_probs = weights / totals
    probs_low = attn_probs.astype(jnp.bfloat16)
    attended = jnp.dot(probs_low, value_rows, preferred_element_type=jnp.float32).astype(
        jnp.bfloat16
    )
    row_dot = jnp.sum(
        grad_rows.astype(jnp.float32) * attended.astype(jnp.float32), axis=1, keepdims=True
    )
    prob_grad = jnp.einsum("rd,kd->rk", grad_rows, value_rows, preferred_element_type=jnp.float32)
    score_grad = (attn_probs * (prob_grad - row_dot)).astype(jnp.bfloat16)
    query_grad = (
        jnp.dot(score_grad, key_rows, preferred_element_type=jnp.float32) * factor
    ).astype(jnp.bfloat16)
    key_part = (
        jnp.einsum("rk,rd->kd", score_grad, head_rows, preferred_element_type=jnp.float32) * factor
    )
    value_part = jnp.einsum("rk,rd->kd", probs_low, grad_rows, preferred_element_type=jnp.float32)
    pair_grad = lax.psum_scatter(
        jnp.concatenate([key_part, value_part], axis=1).astype(jnp.bfloat16),
        "ctx",
        scatter_dimension=0,
        tiled=True,
    ).astype(jnp.float32)
    hidden = residual.reshape(tokens_dev, D).astype(jnp.float32) + jnp.dot(
        attended.reshape(tokens_dev, HQ * HD), w_out, preferred_element_type=jnp.float32
    )
    normed = (
        hidden * lax.rsqrt(jnp.mean(hidden * hidden, axis=1, keepdims=True) + norm_eps) * norm_gain
    ).astype(jnp.bfloat16)
    logits = jnp.dot(normed, w_router, preferred_element_type=jnp.float32)
    experts_all = w_router.shape[1]
    routed = expert_ids.reshape(tokens_dev, TOPK)
    route_match = routed[:, :, None] == jnp.arange(experts_all, dtype=jnp.int32)[None, None, :]
    chosen = jnp.sum(jnp.where(route_match, logits[:, None, :], 0.0), axis=2)
    gate_values = jax.nn.sigmoid(chosen)
    mixing = gate_values / jnp.sum(gate_values, axis=1, keepdims=True)
    if experts_all <= 4 * TOPK and lax.axis_size("dp") == 4 and w_gate_up.shape[0] == 1:
        dense_mix = jnp.sum(jnp.where(route_match, mixing[:, :, None], 0.0), axis=1)
        mixture = gathered_mixture(normed, dense_mix, w_gate_up, w_down)
    else:
        mixture = exchange_mixture(normed, routed, mixing, route_match, w_gate_up, w_down)
    layer_out = (hidden + mixture).astype(jnp.bfloat16).reshape(1, tokens_dev, D)
    return (
        layer_out,
        query_grad.reshape(1, tokens_dev, HQ * HD),
        pair_grad.reshape(1, tokens_dev, 2 * HD),
    )


def solution(mesh):
    placed = (
        P("dp", "ctx", None),
        P("dp", "ctx", None),
        P("dp", "ctx", None),
        P("dp", "ctx", None),
        P(),
        P(),
        P(),
        P("dp", "ctx", None),
        P(("dp", "ctx"), None, None),
        P(("dp", "ctx"), None, None),
    )
    return jax.shard_map(
        shards,
        mesh=mesh,
        in_specs=placed,
        out_specs=(P("dp", "ctx", None), P("dp", "ctx", None), P("dp", "ctx", None)),
        check_vma=False,
    )
```
